256 devices in a mesh: ctx: 32 (over y, x, z_lo), head: 8 (over z_hi, core).
Axes of the slice: x: 4, y: 4, z: 8 (z_hi: 4, z_lo: 2; z = z_hi * 2 + z_lo), core: 2. Of those that a mesh axis runs over, the one named last changes fastest.
Arguments:
- light_query: bfloat16 [16384, 4096], P('ctx', 'head'), may hold values from -6 to 6
- light_key: bfloat16 [16384, 4096], P('ctx', 'head'), may hold values from -6 to 6
- light_value: bfloat16 [16384, 4096], P('ctx', 'head'), may hold values from -6 to 6
- light_gate: bfloat16 [16384, 4096], P('ctx', 'head'), may hold values from -6 to 6
- norm_gain: float32 [4096], P('head'), may hold values from 0.1 to 1.9
- decay_exponent: int32 [32], P('head'), may hold values from 1 to 2048, as said below
- soft_query: bfloat16 [16384, 4096], P('ctx', 'head'), may hold values from -45 to 45
- soft_key: bfloat16 [16384, 4096], P('ctx', 'head'), may hold values from -6 to 6
- soft_value: bfloat16 [16384, 4096], P('ctx', 'head'), may hold values from -6 to 6
Outputs:
- light_output: bfloat16 [16384, 4096], P('ctx', 'head')
- soft_output: bfloat16 [16384, 4096], P('ctx', 'head')
The draws below stay inside these ranges and needn't reach their ends.
Inputs may be any that keep to these rules, and one draw needn't show every extreme that they name: Each head decays by exp(-decay_exponent / 65536) a token; the exponents are powers of two.
All inputs are finite; a program needn't handle non-finite values.
Results may differ from the reference program's by a relative error of at most 0.0096.
Values may be sent and summed in bfloat16 or wider, within the bound.
A program may use at most 128 MiB of HBM per device.

```python
import jax
import jax.numpy as jnp
from jax import lax

HEADS = 32
HD = 128
TOK_DEV = 512
SEQ = 16384


def draw_soft_query(key, part):
    key = jax.random.fold_in(key, 11)
    values = jnp.clip(jax.random.normal(key, (SEQ, HEADS * HD), jnp.float32), -6.0, 6.0)
    return values.astype(jnp.bfloat16)


def draw_soft_key(key, part):
    key = jax.random.fold_in(key, 12)
    values = jnp.clip(jax.random.normal(key, (SEQ, HEADS * HD), jnp.float32), -6.0, 6.0)
    return values.astype(jnp.bfloat16)


def draw_decay_exponent(key, part):
    key = jax.random.fold_in(key, 13)
    order = jax.random.permutation(key, HEADS)
    powers = (order % 12).astype(jnp.int32)
    return jnp.left_shift(jnp.ones((HEADS,), jnp.int32), powers)


def block_levels(rng, dims, pieces, smallest, largest):
    level = 1.0
    for axis_at, blocks in pieces:
        steps = jax.random.uniform(jax.random.fold_in(jax.random.fold_in(rng, 6), axis_at), (blocks,), jnp.float32, smallest / len(pieces), largest / len(pieces))
        level = level * jnp.repeat(jnp.exp(steps), dims[axis_at] // blocks).reshape((-1,) + (1,) * (len(dims) - 1 - axis_at))
    return level


def bell_draw(key, dims, spread, reach, cuts=(), kind=jnp.bfloat16):
    loudness = block_levels(key, dims, cuts, -0.22, 0.18) if cuts else 1.0
    values = jax.random.normal(key, dims, jnp.float32) * spread * loudness
    return jnp.minimum(jnp.maximum(values, -reach), reach).astype(kind)


def setup_inputs(seed: int = 0) -> dict:
    splits = jax.random.split(jax.random.key(seed), 10)
    return {
        "light_query": bell_draw(splits[0], (SEQ, HEADS * HD), 1.0, 6.0, ((0, 32), (1, 8))),
        "light_key": bell_draw(splits[1], (SEQ, HEADS * HD), 1.0, 6.0, ((0, 32), (1, 8))),
        "light_value": bell_draw(splits[2], (SEQ, HEADS * HD), 1.0, 6.0, ((0, 32), (1, 8))),
        "light_gate": bell_draw(splits[3], (SEQ, HEADS * HD), 1.5, 6.0, ((0, 32), (1, 8))),
        "norm_gain": jnp.clip(1.0 + 0.18 * jax.random.normal(splits[4], (HEADS * HD,), jnp.float32), 0.1, 1.9),
        "decay_exponent": draw_decay_exponent(jax.random.fold_in(splits[9], 71), 0),
        "soft_query": draw_soft_query(jax.random.fold_in(splits[9], 71), 0),
        "soft_key": draw_soft_key(jax.random.fold_in(splits[9], 71), 0),
        "soft_value": bell_draw(splits[8], (SEQ, HEADS * HD), 1.0, 6.0, ((0, 32), (1, 8))),
    }


def lightning(light_query, light_key, light_value, log_decay):
    blocks = SEQ // TOK_DEV
    shape = (blocks, TOK_DEV, HEADS, HD)
    positions = jnp.arange(TOK_DEV, dtype=jnp.float32)
    offsets = positions[:, None] - positions[None, :]
    decay_mask = jnp.where(offsets[None] >= 0, jnp.exp(jnp.maximum(offsets, 0.0)[None] * log_decay[:, None, None]), 0.0)
    row_decay = jnp.exp((positions + 1.0)[:, None] * log_decay[None, :])
    key_decay = jnp.exp((TOK_DEV - 1.0 - positions)[:, None] * log_decay[None, :])
    block_factor = jnp.exp(TOK_DEV * log_decay)

    def advance(state, inputs):
        query_block, key_block, value_block = inputs
        query_float = query_block.astype(jnp.float32)
        key_float = key_block.astype(jnp.float32)
        value_float = value_block.astype(jnp.float32)
        scores = jnp.einsum('thd,shd->hts', query_float, key_float)
        weighted = (scores * decay_mask).astype(jnp.bfloat16)
        intra = jnp.einsum('hts,she->the', weighted.astype(jnp.float32), value_float)
        inter = jnp.einsum('thd,hde->the', query_float, state, precision=lax.Precision.HIGHEST)
        mixed = intra + row_decay[:, :, None] * inter
        local_state = jnp.einsum('shd,she->hde', key_float * key_decay[:, :, None], value_float, precision=lax.Precision.HIGHEST)
        return (block_factor[:, None, None] * state + local_state, mixed)
    start_state = jnp.zeros((HEADS, HD, HD), jnp.float32)
    unused, mixed = lax.scan(advance, start_state, (light_query.reshape(shape), light_key.reshape(shape), light_value.reshape(shape)))
    return mixed.reshape(SEQ, HEADS * HD)

def softmax_layer(soft_query, soft_key, soft_value):
    blocks = SEQ // TOK_DEV
    scale = HD ** (-0.5)
    query_heads = soft_query.reshape(SEQ, HEADS, HD).transpose(1, 0, 2)
    key_heads = soft_key.reshape(SEQ, HEADS, HD).transpose(1, 0, 2)
    value_heads = soft_value.reshape(SEQ, HEADS, HD).transpose(1, 0, 2)
    key_positions = jnp.arange(SEQ, dtype=jnp.int32)

    def one_head(inputs):
        query_head, key_head, value_head = inputs

        def one_block(block_inputs):
            query_block, block_index = block_inputs
            query_positions = block_index * TOK_DEV + jnp.arange(TOK_DEV, dtype=jnp.int32)
            causal = query_positions[:, None] >= key_positions[None, :]
            scores = jnp.dot(query_block, key_head.T, preferred_element_type=jnp.float32) * scale
            scores = jnp.where(causal, scores, -1e+30)
            row_max = lax.optimization_barrier(jnp.max(scores, axis=1, keepdims=True))
            expo = jnp.where(causal, jnp.exp(scores - row_max), 0.0)
            total = lax.optimization_barrier(jnp.sum(expo, axis=1, keepdims=True))
            probs = expo.astype(jnp.bfloat16)
            result = jnp.dot(probs, value_head, preferred_element_type=jnp.float32) / total
            return result.astype(jnp.bfloat16)
        return lax.map(one_block, (query_head.reshape(blocks, TOK_DEV, HD), jnp.arange(blocks, dtype=jnp.int32)))
    outputs = lax.map(one_head, (query_heads, key_heads, value_heads))
    return outputs.reshape(HEADS, SEQ, HD).transpose(1, 0, 2).reshape(SEQ, HEADS * HD)

def reference(light_query, light_key, light_value, light_gate, norm_gain, decay_exponent, soft_query, soft_key, soft_value):
    log_decay = -decay_exponent.astype(jnp.float32) / 65536.0
    mixed = lightning(light_query, light_key, light_value, log_decay)
    mean_square = lax.optimization_barrier(jnp.mean(mixed * mixed, axis=1, keepdims=True))
    light_output = (mixed * lax.rsqrt(mean_square + 1e-05) * norm_gain[None, :] * jax.nn.sigmoid(light_gate.astype(jnp.float32))).astype(jnp.bfloat16)
    soft_output = softmax_layer(soft_query, soft_key, soft_value)
    return (light_output, soft_output)
```

```python
import jax
import jax.numpy as jnp
from jax import lax
from jax.experimental import pallas as pl
from jax.experimental.pallas import tpu as pltpu
from jax.sharding import PartitionSpec as P

HEADS = 32
HD = 128
TOK = 512
MESH = pl.DeviceIdType.MESH
SCALE2 = HD**-0.5 * 1.4426950408889634
QT = 256
f32 = jnp.float32
bf16 = jnp.bfloat16


def dot_nt(a, b):
    return lax.dot_general(a, b, (((1,), (1,)), ((), ())), preferred_element_type=f32)


def dot_tn(a, b):
    return lax.dot_general(a, b, (((0,), (0,)), ((), ())), preferred_element_type=f32)


def kernel(
    lq, lk, lv, lg, gain, ld_ref, sq, sk, sv,
    lo, so,
    kv, qb, ob, m_ref, acc, mixed, st_send, st_recv, car_send, car_recv, ss_send, ss_recv,
    kv_sem, p1_sem, q_sem, q_send, fwd_sem, o_sem, o_send,
    st_ssem, st_rsem, car_ssem, car_rsem, ss_ssem, ss_rsem,
):
    c = lax.axis_index("ctx")
    h = lax.axis_index("head")
    y, x, zl = c // 8, (c // 2) % 4, c % 2
    zh, core = h // 2, h % 2
    slot = 2 * x + core

    def remote(src, dst, ssem, rsem, ctx, head):
        return pltpu.make_async_remote_copy(
            src_ref=src, dst_ref=dst, send_sem=ssem, recv_sem=rsem,
            device_id=(ctx, head), device_id_type=MESH,
        )

    def arrived(ref, sem):
        pltpu.make_async_copy(ref, ref, sem).wait()

    barrier = pltpu.get_barrier_semaphore()

    def hello(i, carry):
        pl.semaphore_signal(
            barrier, 1,
            device_id=((c + i // 2) % 32, zh * 2 + (core + i) % 2),
            device_id_type=MESH,
        )
        return carry

    lax.fori_loop(1, 64, hello, 0)

    def hello_head(i, carry):
        pl.semaphore_signal(barrier, 1, device_id=(c, (h + i) % 8), device_id_type=MESH)
        return carry

    lax.fori_loop(2 - core, 8 - core, hello_head, 0)
    pl.semaphore_wait(barrier, 69)

    odd = y % 2
    q_x = jnp.where(odd == 1, 3 - x, x)
    q_core = jnp.where(odd == 1, 1 - zl, zl)
    first = []
    for a in range(4):
        cols = pl.ds(a * HD, HD)
        for part, src in ((0, sk), (1, sv)):
            here = (a == y) & (core == zl)
            dst = kv.at[y, 2 * x + zl, part]
            sem = kv_sem.at[y, 2 * x + zl, part]
            first.append((here, remote(src.at[:, cols], dst, p1_sem.at[a, part], sem, a * 8 + x * 2 + core, zh * 2 + zl),
                          pltpu.make_async_copy(src.at[:, cols], dst, sem)))
    for a in range(4):
        cols = pl.ds(a * HD, HD)
        here = (a == y) & (core == zl) & (odd == 0)
        first.append((here, remote(sq.at[:, cols], qb.at[y], q_send.at[a], q_sem.at[y], a * 8 + q_x * 2 + core, zh * 2 + q_core),
                      pltpu.make_async_copy(sq.at[:, cols], qb.at[y], q_sem.at[y])))
    for here, far, near in first:
        @pl.when(here)
        def _():
            near.start()

        @pl.when(jnp.logical_not(here))
        def _():
            far.start()

    right = y * 8 + ((x + 1) % 4) * 2 + zl
    left = y * 8 + ((x + 3) % 4) * 2 + zl
    sib = zh * 2 + 1 - core

    def block(d):
        return 2 * ((x + d) % 4) + core

    def other(d):
        return 2 * ((x + d) % 4) + 1 - core

    def forward(s, b, ctx, head):
        remote(kv.at[s, b], kv.at[s, b], fwd_sem.at[s], kv_sem.at[s, b, 0], ctx, head).start()

    def own_piece(s):
        b = block(0)
        arrived(kv.at[s, b, 0], kv_sem.at[s, b, 0])
        arrived(kv.at[s, b, 1], kv_sem.at[s, b, 1])
        forward(s, b, right, h)
        forward(s, b, left, h)
        forward(s, b, c, sib)

    def from_sides(s):
        for d, part, ctx in ((3, 0, right), (1, 1, left)):
            b = block(d)
            arrived(kv.at[s, b], kv_sem.at[s, b, 0])
            remote(kv.at[s, b, part], kv.at[s, b, part], fwd_sem.at[s], kv_sem.at[s, b, part], ctx, h).start()
            forward(s, b, c, sib)

    def from_far(s):
        b = block(2)
        arrived(kv.at[s, b, 0], kv_sem.at[s, b, 0])
        arrived(kv.at[s, b, 1], kv_sem.at[s, b, 1])
        forward(s, b, c, sib)

    def from_sibling(s, d):
        b = other(d)
        arrived(kv.at[s, b], kv_sem.at[s, b, 0])

    def slice_at(k):
        return jnp.where(k == 0, y, jnp.where(k - 1 < y, k - 1, k))

    rows = lax.broadcasted_iota(jnp.int32, (TOK, HD), 0).astype(f32)

    def head_cols(a):
        return pl.ds(pl.multiple_of(a * HD, HD), HD)

    def states(a, carry):
        cols = head_cols(a)
        ld = ld_ref[a][:1, :]
        kd = (lk[:, cols].astype(f32) * jnp.exp((TOK - 1.0 - rows) * ld)).astype(bf16)
        st_send[head_cols(a), :] = dot_tn(kd, lv[:, cols]).astype(bf16)
        return carry

    lax.fori_loop(0, 4, states, 0)

    def scan_rows(i):
        return pl.ds(pl.multiple_of(i * 16, 16), 16)

    def send_state(i, carry):
        to = (c + i) % 32
        remote(st_send.at[scan_rows(to)], st_recv.at[scan_rows(c)], st_ssem, st_rsem, to, h).start()
        return carry

    lax.fori_loop(1, 32, send_state, 0)
    pltpu.make_async_copy(st_send.at[scan_rows(c)], st_recv.at[scan_rows(c)], st_rsem).start()

    own_piece(y)

    def intra(a, carry):
        cols = head_cols(a)
        ld = ld_ref[a][:1, :1]
        k = lk[:, cols]
        v = lv[:, cols]
        for i in range(2):
            n = (i + 1) * 256
            t = i * 256 + lax.broadcasted_iota(jnp.int32, (256, n), 0)
            s = lax.broadcasted_iota(jnp.int32, (256, n), 1)
            up = jnp.exp((i * 256 + lax.broadcasted_iota(jnp.int32, (256, 1), 0)).astype(f32) * ld)
            down = jnp.exp(-lax.broadcasted_iota(jnp.int32, (1, n), 1).astype(f32) * ld)
            w = dot_nt(lq[pl.ds(i * 256, 256), cols], k[:n]) * up * down
            w = jnp.where(t >= s, w, 0.0).astype(bf16)
            mixed[pl.ds(i * 256, 256), cols] = jnp.dot(w, v[:n], preferred_element_type=f32)
        return carry

    lax.fori_loop(0, 4, intra, 0)

    def scan_states():
        arrived(st_recv, st_rsem)
        f = jnp.exp(TOK * ld_ref[c // 8][:1, :])

        def step(b, carry):
            car_send[scan_rows(b), :] = carry.astype(bf16)
            return carry * f + st_recv[scan_rows(b), :].astype(f32)

        lax.fori_loop(0, 32, step, jnp.zeros((16, HD), f32))

        def send_carried(i, carry):
            to = (c + i) % 32
            remote(car_send.at[scan_rows(to)], car_recv.at[scan_rows(c)], car_ssem, car_rsem, to, h).start()
            return carry

        lax.fori_loop(1, 32, send_carried, 0)
        pltpu.make_async_copy(car_send.at[scan_rows(c)], car_recv.at[scan_rows(c)], car_rsem).start()

    def add_inter():
        arrived(car_recv, car_rsem)

        def one(a, squares):
            cols = head_cols(a)
            ld = ld_ref[a][:1, :]
            inter = jnp.dot(lq[:, cols], car_recv[head_cols(a), :], preferred_element_type=f32)
            both = mixed[:, cols] + jnp.exp((rows + 1.0) * ld) * inter
            mixed[:, cols] = both
            return squares + both * both

        squares = lax.fori_loop(0, 4, one, jnp.zeros((TOK, HD), f32))
        total = jnp.sum(squares.T, axis=0, keepdims=True)
        ss_send[...] = jnp.broadcast_to(total, (8, TOK))
        ss_recv[h] = ss_send[...]

        def send_squares(i, carry):
            remote(ss_send, ss_recv.at[h], ss_ssem, ss_rsem, c, (h + i) % 8).start()
            return carry

        lax.fori_loop(1, 8, send_squares, 0)

    def finish_light():
        arrived(ss_recv.at[pl.ds(0, 7)], ss_rsem)
        total = jnp.sum(ss_recv[...], axis=0)[:1, :]
        scale = lax.rsqrt(total / (HEADS * HD) + 1e-5)
        scale = jnp.broadcast_to(scale, (HD, TOK)).T
        for a in range(4):
            cols = pl.ds(a * HD, HD)
            gate = lg[:, cols].astype(f32)
            lo[:, cols] = (mixed[:, cols] * scale * gain[:, cols] / (1.0 + jnp.exp(-gate))).astype(bf16)

    m_ref[...] = jnp.full_like(m_ref, -1e30)
    acc[...] = jnp.zeros_like(acc)

    def tile(k, v, yq, q_at=None, k_at=None):
        n = k.shape[0]
        v2 = jnp.concatenate([v, jnp.ones_like(v)], axis=1)
        for i in range(TOK // QT):
            sl = pl.ds(i * QT, QT)
            s = dot_nt(qb[yq, sl, :], k)
            if q_at is not None:
                t = q_at + i * QT + lax.broadcasted_iota(jnp.int32, (QT, n), 0)
                j = k_at + lax.broadcasted_iota(jnp.int32, (QT, n), 1)
                s = jnp.where(t >= j, s, -1e30)
            old = m_ref[yq, sl, :]
            new = jnp.maximum(old, jnp.max(s, axis=1, keepdims=True))
            p = jnp.exp2((s - new[:, :1]) * SCALE2).astype(bf16)
            shrink = jnp.exp2((old - new) * SCALE2)
            acc[yq, sl, :] = acc[yq, sl, :] * jnp.concatenate([shrink, shrink], axis=1) + jnp.dot(
                p, v2, preferred_element_type=f32
            )
            m_ref[yq, sl, :] = new

    def pair(s, b):
        k = kv[s, pl.ds(2 * b, 2), 0].reshape(2 * TOK, HD)
        v = kv[s, pl.ds(2 * b, 2), 1].reshape(2 * TOK, HD)
        return k, v

    def full(s, d):
        def one(yq, carry):
            k, v = pair(s, (x + d) % 4)
            tile(k, v, yq)
            return carry

        lax.fori_loop(s + 1, 4, one, 0)

    def diagonal(s):
        r = jnp.where(s % 2 == 1, 7 - slot, slot)

        def one(b, carry):
            k, v = pair(s, b)
            tile(k, v, s)
            return carry

        lax.fori_loop(0, r // 2, one, 0)
        k, v = pair(s, r // 2)
        tile(k, v, s, r * TOK, (r // 2) * 2 * TOK)

    def o_copy(yq):
        ox = jnp.where(yq % 2 == 1, 3 - x, x)
        oz = jnp.where(yq % 2 == 1, 1 - core, core)
        here = (yq == y) & (core == zl) & (yq % 2 == 0)
        dst = so.at[:, head_cols(y)]
        far = remote(ob.at[yq], dst, o_send.at[yq], o_sem.at[y], yq * 8 + ox * 2 + oz, zh * 2 + zl)
        return here, far, pltpu.make_async_copy(ob.at[yq], dst, o_sem.at[y])

    def finish(yq):
        for i in range(TOK // QT):
            sl = pl.ds(i * QT, QT)
            ob[yq, sl, :] = (acc[yq, sl, :HD] / acc[yq, sl, HD:]).astype(bf16)
        here, far, near = o_copy(yq)

        @pl.when(here)
        def _():
            near.start()

        @pl.when(jnp.logical_not(here))
        def _():
            far.start()

    for i in range(4):
        arrived(qb.at[i], q_sem.at[i])

    def step(k, carry):
        s = slice_at(k)
        from_sibling(s, 0)
        full(s, 0)
        from_sides(s)

        @pl.when(k < 3)
        def _():
            own_piece(slice_at(k + 1))

        from_sibling(s, 3)
        full(s, 3)
        from_sibling(s, 1)
        full(s, 1)
        from_far(s)

        @pl.when(k == 0)
        def _():
            scan_states()

        @pl.when(k == 1)
        def _():
            add_inter()

        @pl.when(k == 2)
        def _():
            finish_light()

        from_sibling(s, 2)
        full(s, 2)
        diagonal(s)

        @pl.when((k >= 1) & (k <= y))
        def _():
            finish(k - 1)

        @pl.when(k >= y)
        def _():
            finish(k)

        return carry

    lax.fori_loop(0, 4, step, 0)

    for a in range(4):
        arrived(so.at[:, pl.ds(a * HD, HD)], o_sem.at[a])
        arrived(kv.at[a, pl.ds(0, 7)], fwd_sem.at[a])
        here, far, near = o_copy(a)

        @pl.when(jnp.logical_not(here))
        def _():
            far.wait_send()

    for here, far, near in first:
        @pl.when(jnp.logical_not(here))
        def _():
            far.wait_send()

    arrived(st_send.at[pl.ds(0, 31 * 16)], st_ssem)
    arrived(car_send.at[pl.ds(0, 31 * 16)], car_ssem)
    arrived(ss_recv.at[pl.ds(0, 7)], ss_ssem)


def body(lq, lk, lv, lg, gain, decay_exponent, sq, sk, sv):
    log_decay = -decay_exponent.astype(f32) / 65536.0
    ld = jnp.broadcast_to(log_decay[:, None, None], (4, 8, HD))
    vmem = pl.BlockSpec(memory_space=pltpu.VMEM)
    anywhere = pl.BlockSpec(memory_space=pl.ANY)
    dma = pltpu.SemaphoreType.DMA
    out = jax.ShapeDtypeStruct((TOK, 4 * HD), bf16)
    return pl.pallas_call(
        kernel,
        out_shape=(out, out),
        in_specs=[vmem] * 6 + [anywhere] * 3,
        out_specs=(vmem, anywhere),
        scratch_shapes=[
            pltpu.VMEM((4, 8, 2, TOK, HD), bf16),
            pltpu.VMEM((4, TOK, HD), bf16),
            pltpu.VMEM((4, TOK, HD), bf16),
            pltpu.VMEM((4, TOK, HD), f32),
            pltpu.VMEM((4, TOK, 2 * HD), f32),
            pltpu.VMEM((TOK, 4 * HD), f32),
            pltpu.VMEM((TOK, HD), bf16),
            pltpu.VMEM((TOK, HD), bf16),
            pltpu.VMEM((TOK, HD), bf16),
            pltpu.VMEM((TOK, HD), bf16),
            pltpu.VMEM((8, TOK), f32),
            pltpu.VMEM((8, 8, TOK), f32),
            dma((4, 8, 2)), dma((4, 2)), dma((4,)), dma((4,)), dma((4,)), dma((4,)), dma((4,)),
            dma, dma, dma, dma, dma, dma,
        ],
        compiler_params=pltpu.CompilerParams(
            collective_id=0, has_side_effects=True, vmem_limit_bytes=48 * 1024 * 1024
        ),
        name="layers",
    )(lq, lk, lv, lg, gain[None, :], ld, sq, sk, sv)


def solution(mesh):
    spec = P("ctx", "head")
    return jax.shard_map(
        body,
        mesh=mesh,
        in_specs=(spec, spec, spec, spec, P("head"), P("head"), spec, spec, spec),
        out_specs=(spec, spec),
        check_vma=False,
    )
```

```python
import jax
import jax.numpy as jnp
from jax import lax
from jax.experimental import pallas as pl
from jax.experimental.pallas import tpu as pltpu
from jax.sharding import PartitionSpec as P

HEADS = 32
HD = 128
TOK = 512
MESH = pl.DeviceIdType.MESH
SCALE2 = HD**-0.5 * 1.4426950408889634
QT = 128
f32 = jnp.float32
bf16 = jnp.bfloat16


def dot_nt(a, b):
    return lax.dot_general(a, b, (((1,), (1,)), ((), ())), preferred_element_type=f32)


def dot_tn(a, b):
    return lax.dot_general(a, b, (((0,), (0,)), ((), ())), preferred_element_type=f32)


def kernel(
    lq_h, lk_h, lv_h, lg_h, gain, ld_ref, sq_h, sk_h, sv_h,
    lo, so,
    lq, lk, lv, lg, sq, sk, sv,
    kv, qb, ob, ol, m_ref, acc, mixed, home, home_l, o_in, l_in,
    st_send, st_recv, car_send, car_recv, ss_send, ss_recv,
    load_sem, kv_sem, p1_sem, q_sem, q_send, q_fwd, fwd_sem, o_sem, l_sem, o_send, l_send,
    st_ssem, st_rsem, car_ssem, car_rsem, ss_ssem, ss_rsem,
):
    c = lax.axis_index("ctx")
    h = lax.axis_index("head")
    y, x, zl = c // 8, (c // 2) % 4, c % 2
    zh, core = h // 2, h % 2
    sib = zh * 2 + 1 - core
    half = x // 2
    par = x % 2

    def remote(src, dst, ssem, rsem, ctx, head):
        return pltpu.make_async_remote_copy(
            src_ref=src, dst_ref=dst, send_sem=ssem, recv_sem=rsem,
            device_id=(ctx, head), device_id_type=MESH,
        )

    def arrived(ref, sem):
        pltpu.make_async_copy(ref, ref, sem).wait()

    def queries(n):
        return qb.at[n // 2, pl.ds(pl.multiple_of(n % 2 * TOK, TOK), TOK)]

    def head_cols(a):
        return pl.ds(pl.multiple_of(a * HD, HD), HD)

    barrier = pltpu.get_barrier_semaphore()

    def hello(i, carry):
        pl.semaphore_signal(
            barrier, 1,
            device_id=((c + i // 2) % 32, zh * 2 + (core + i) % 2),
            device_id_type=MESH,
        )
        return carry

    lax.fori_loop(1, 64, hello, 0)

    def hello_head(i, carry):
        pl.semaphore_signal(barrier, 1, device_id=(c, (h + i) % 8), device_id_type=MESH)
        return carry

    lax.fori_loop(2 - core, 8 - core, hello_head, 0)

    loads = [
        pltpu.make_async_copy(src, dst, load_sem.at[n])
        for n, (src, dst) in enumerate(
            ((lk_h, lk), (lv_h, lv), (lq_h, lq), (sq_h, sq), (sk_h, sk), (sv_h, sv), (lg_h, lg))
        )
    ]
    for load in loads:
        load.start()

    rows = lax.broadcasted_iota(jnp.int32, (TOK, HD), 0).astype(f32)
    loads[0].wait()
    loads[1].wait()

    for a in range(4):
        cols = pl.ds(a * HD, HD)
        ld = ld_ref[a][:1, :]
        kd = (lk[:, cols].astype(f32) * jnp.exp((TOK - 1.0 - rows) * ld)).astype(bf16)
        st_send[cols, :] = dot_tn(kd, lv[:, cols]).astype(bf16)

    m_ref[...] = jnp.full_like(m_ref, -1e30)
    acc[...] = jnp.zeros_like(acc)

    pl.semaphore_wait(barrier, 69)

    odd = y % 2
    q_x = jnp.where(odd == 1, 3 - x, x)
    q_core = jnp.where(odd == 1, 1 - zl, zl)
    q_at = 2 * y + q_x % 2

    def kv_copy(i, part):
        a = (y + i) % 4
        src = (sk_h, sv_h)[part].at[:, head_cols(a)]
        dst = kv.at[y, 2 * half + zl, part]
        sem = kv_sem.at[y, 2 * half + zl, part]
        zd = (core + a) % 2
        far = remote(src, dst, p1_sem.at[i, part], sem, a * 8 + x * 2 + zd, zh * 2 + zl)
        return (i == 0) & (zd == zl) & (core == zl), far, pltpu.make_async_copy(src, dst, sem)

    def q_copy(i):
        a = (y + i) % 4
        src = sq_h.at[:, head_cols(a)]
        dst, sem = queries(q_at), q_sem.at[q_at]
        zd = (core + a) % 2
        far = remote(src, dst, q_send.at[i], sem, a * 8 + q_x * 2 + zd, zh * 2 + q_core)
        return (i == 0) & (zd == zl) & (core == zl) & (odd == 0), far, pltpu.make_async_copy(src, dst, sem)

    def start(copy):
        here, far, near = copy

        @pl.when(here)
        def _():
            near.start()

        @pl.when(jnp.logical_not(here))
        def _():
            far.start()

    def wait_sent(copy):
        here, far, near = copy

        @pl.when(jnp.logical_not(here))
        def _():
            far.wait_send()

    start(kv_copy(0, 0))
    start(kv_copy(0, 1))
    for i in (0, 3, 2):
        start(q_copy(i))

    def scan_rows(i):
        return pl.ds(pl.multiple_of(i * 16, 16), 16)

    def send_state(i, carry):
        to = (c + i) % 32
        remote(st_send.at[scan_rows(to)], st_recv.at[scan_rows(c)], st_ssem, st_rsem, to, h).start()
        return carry

    lax.fori_loop(1, 32, send_state, 0)
    pltpu.make_async_copy(st_send.at[scan_rows(c)], st_recv.at[scan_rows(c)], st_rsem).start()

    loads[2].wait()

    def intra(heads):
        units = [(a, i) for a in heads for i in range(2)]

        def scores(a, i):
            cols = pl.ds(a * HD, HD)
            return dot_nt(lq[pl.ds(i * 256, 256), cols], lk[pl.ds(0, (i + 1) * 256), cols])

        s = scores(*units[0])
        for at, (a, i) in enumerate(units):
            ahead = scores(*units[at + 1]) if at + 1 < len(units) else None
            n = (i + 1) * 256
            cols = pl.ds(a * HD, HD)
            ld = ld_ref[a][:1, :1]
            t = i * 256 + lax.broadcasted_iota(jnp.int32, (256, n), 0)
            j = lax.broadcasted_iota(jnp.int32, (256, n), 1)
            up = jnp.exp((i * 256 + lax.broadcasted_iota(jnp.int32, (256, 1), 0)).astype(f32) * ld)
            down = jnp.exp(-lax.broadcasted_iota(jnp.int32, (1, n), 1).astype(f32) * ld)
            w = jnp.where(t >= j, s * up * down, 0.0).astype(bf16)
            mixed[pl.ds(i * 256, 256), cols] = jnp.dot(w, lv[pl.ds(0, n), cols], preferred_element_type=f32)
            s = ahead

    intra((0, 1, 2, 3))

    start(q_copy(1))
    start(kv_copy(3, 0))
    start(kv_copy(3, 1))

    def own_piece(s):
        b = 2 * half + core
        arrived(kv.at[s, b, 0], kv_sem.at[s, b, 0])
        arrived(kv.at[s, b, 1], kv_sem.at[s, b, 1])
        remote(kv.at[s, b], kv.at[s, b], fwd_sem.at[s], kv_sem.at[s, b, 0], y * 8 + (3 - x) * 2 + zl, h).start()
        remote(kv.at[s, b], kv.at[s, b], fwd_sem.at[s], kv_sem.at[s, b, 0], c, sib).start()

    def paired_piece(s):
        b = 2 * (1 - half) + core
        arrived(kv.at[s, b], kv_sem.at[s, b, 0])
        remote(kv.at[s, b], kv.at[s, b], fwd_sem.at[s], kv_sem.at[s, b, 0], c, sib).start()

    def slice_at(j):
        return (y + jnp.where(j == 2, 3, jnp.where(j == 3, 2, j))) % 4

    def place_of(s):
        d = (s - y + 4) % 4
        return jnp.where(d == 2, 3, jnp.where(d == 3, 2, d))

    own_piece(y)

    for n in (3, 4, 5):
        loads[n].wait()

    def at_home(heads):
        units = [(a, i) for a in heads for i in range(2)]

        def scores(a, i):
            cols = pl.ds(a * HD, HD)
            return dot_nt(sq[pl.ds(i * 256, 256), cols], sk[pl.ds(0, (i + 1) * 256), cols])

        s = scores(*units[0])
        for at, (a, i) in enumerate(units):
            ahead = scores(*units[at + 1]) if at + 1 < len(units) else None
            n = (i + 1) * 256
            sl = pl.ds(i * 256, 256)
            t = i * 256 + lax.broadcasted_iota(jnp.int32, (256, n), 0)
            j = lax.broadcasted_iota(jnp.int32, (256, n), 1)
            s = jnp.where(t >= j, s, -1e30)
            top = jnp.max(s, axis=1, keepdims=True)
            p = jnp.exp2((s - top) * SCALE2).astype(bf16)
            v = sv[pl.ds(0, n), pl.ds(a * HD, HD)]
            o = jnp.dot(p, jnp.concatenate([v, jnp.ones_like(v)], axis=1), preferred_element_type=f32)
            home[a, sl, :] = o[:, :HD] / o[:, HD:]
            home_l[a, sl, :] = top * SCALE2 + jnp.log2(o[:, HD:])
            s = ahead

    def pass_queries(i):
        yq = (y + i) % 4
        n = 2 * yq + par
        arrived(queries(n), q_sem.at[n])
        remote(queries(n), queries(n), q_fwd.at[i], q_sem.at[n], y * 8 + (x + 1 - 2 * par) * 2 + zl, h).start()

    at_home((0, 1))
    start(kv_copy(1, 0))
    start(kv_copy(1, 1))
    pass_queries(0)
    pass_queries(1)
    at_home((2, 3))
    start(kv_copy(2, 0))
    start(kv_copy(2, 1))
    pass_queries(2)
    pass_queries(3)

    def scan_states():
        arrived(st_recv, st_rsem)
        f = jnp.exp(TOK * ld_ref[c // 8][:1, :])

        def step(b, carry):
            car_send[scan_rows(b), :] = carry.astype(bf16)
            return carry * f + st_recv[scan_rows(b), :].astype(f32)

        lax.fori_loop(0, 32, step, jnp.zeros((16, HD), f32))

        def send_carried(i, carry):
            to = (c + i) % 32
            remote(car_send.at[scan_rows(to)], car_recv.at[scan_rows(c)], car_ssem, car_rsem, to, h).start()
            return carry

        lax.fori_loop(1, 32, send_carried, 0)
        pltpu.make_async_copy(car_send.at[scan_rows(c)], car_recv.at[scan_rows(c)], car_rsem).start()

    def add_inter():
        arrived(car_recv, car_rsem)

        def one(a, squares):
            cols = head_cols(a)
            ld = ld_ref[a][:1, :]
            inter = jnp.dot(lq[:, cols], car_recv[head_cols(a), :], preferred_element_type=f32)
            both = mixed[:, cols] + jnp.exp((rows + 1.0) * ld) * inter
            mixed[:, cols] = both
            return squares + both * both

        squares = lax.fori_loop(0, 4, one, jnp.zeros((TOK, HD), f32))
        total = jnp.sum(squares.T, axis=0, keepdims=True)
        ss_send[...] = jnp.broadcast_to(total, (8, TOK))
        ss_recv[h] = ss_send[...]

        def send_squares(i, carry):
            remote(ss_send, ss_recv.at[h], ss_ssem, ss_rsem, c, (h + i) % 8).start()
            return carry

        lax.fori_loop(1, 8, send_squares, 0)

    def finish_light():
        arrived(ss_recv.at[pl.ds(0, 7)], ss_rsem)
        loads[6].wait()
        total = jnp.sum(ss_recv[...], axis=0)[:1, :]
        scale = lax.rsqrt(total / (HEADS * HD) + 1e-5)
        scale = jnp.broadcast_to(scale, (HD, TOK)).T
        for a in range(4):
            cols = pl.ds(a * HD, HD)
            gate = lg[:, cols].astype(f32)
            lo[:, cols] = (mixed[:, cols] * scale * gain[:, cols] / (1.0 + jnp.exp(-gate))).astype(bf16)


    scan_states()
    own_piece(slice_at(1))

    def tile(k, v, yq, start_row, count):
        v2 = jnp.concatenate([v, jnp.ones_like(v)], axis=1)

        def piece(i):
            return pl.ds(start_row + i * QT, QT)

        def scores(i):
            return dot_nt(qb[yq, piece(i), :], k)

        def add(i, p, shrink):
            acc[yq, piece(i), :] = acc[yq, piece(i), :] * jnp.concatenate([shrink, shrink], axis=1) + jnp.dot(
                p, v2, preferred_element_type=f32
            )

        s = scores(0)
        behind = None
        for i in range(count // QT):
            ahead = scores(i + 1) if (i + 1) * QT < count else None
            old = m_ref[yq, piece(i), :]
            new = jnp.maximum(old, jnp.max(s, axis=1, keepdims=True))
            p = jnp.exp2((s - new[:, :1]) * SCALE2).astype(bf16)
            shrink = jnp.exp2((old - new) * SCALE2)
            m_ref[yq, piece(i), :] = new
            if behind is not None:
                add(*behind)
            behind = (i, p, shrink)
            s = ahead
        add(*behind)

    def query_home(n):
        yq, xd = n // 2, 2 * half + n % 2
        return jnp.where(yq % 2 == 1, 3 - xd, xd), jnp.where(yq % 2 == 1, 1 - core, core)

    def o_copies(n):
        yq = n // 2
        ox, oz = query_home(n)
        from_core = (zl + y) % 2
        here = (yq == y) & (ox == x) & (oz == zl) & (core == from_core)
        ctx, head = yq * 8 + ox * 2 + oz, zh * 2 + from_core
        return [
            (here, remote(src.at[n], dst.at[y, par], ssem.at[n], rsem.at[y, par], ctx, head),
             pltpu.make_async_copy(src.at[n], dst.at[y, par], rsem.at[y, par]))
            for src, dst, ssem, rsem in ((ob, o_in, o_send, o_sem), (ol, l_in, l_send, l_sem))
        ]

    def finish(n):
        yq, base = n // 2, pl.multiple_of(n % 2 * TOK, TOK)
        for i in range(2):
            sl, at = pl.ds(i * 256, 256), pl.ds(base + i * 256, 256)
            total = acc[yq, at, HD:]
            some = jnp.maximum(total, 1e-30)
            ob[n, sl, :] = (acc[yq, at, :HD] / some).astype(bf16)
            lse = jnp.where(total > 0.0, m_ref[yq, at, :] * SCALE2 + jnp.log2(some), -1e30)
            ol[n, :, sl] = lse.T[:8, :]
        for copy in o_copies(n):
            start(copy)

    paired_piece(y)

    def step(j, carry):
        s = slice_at(j)
        for part in range(2):
            b = 2 * part + 1 - core
            arrived(kv.at[s, b], kv_sem.at[s, b, 0])

        def one(i, carry):
            yq = (y + 1 + i) % 4

            @pl.when(j == 0)
            def _():
                n = 2 * yq + 1 - par
                arrived(queries(n), q_sem.at[n])

            @pl.when((i == 1) & (j < 2))
            def _():
                own_piece(slice_at(j + 2))

            @pl.when((i == 3) & (j < 3))
            def _():
                paired_piece(slice_at(j + 1))

            @pl.when((i == 2) & (j == 0))
            def _():
                add_inter()

            @pl.when((i == 2) & (j == 1))
            def _():
                finish_light()

            @pl.when(s < yq)
            def _():
                k = kv[s, :, 0].reshape(4 * TOK, HD)
                v = kv[s, :, 1].reshape(4 * TOK, HD)
                tile(k, v, yq, 0, 2 * TOK)

            @pl.when(s == yq)
            def _():
                def some(e, carry):
                    n, at = 2 * yq + e // 2, e % 2
                    xk = jnp.where(at == half, x, 3 - x)
                    row = pl.multiple_of(e // 2 * TOK, TOK)
                    ox, oz = query_home(n)

                    @pl.when(xk < ox)
                    def _():
                        k = kv[s, pl.ds(2 * at, 2), 0].reshape(2 * TOK, HD)
                        v = kv[s, pl.ds(2 * at, 2), 1].reshape(2 * TOK, HD)
                        tile(k, v, yq, row, TOK)

                    @pl.when((xk == ox) & (oz == 1))
                    def _():
                        tile(kv[s, 2 * at, 0], kv[s, 2 * at, 1], yq, row, TOK)

                    return carry

                lax.fori_loop(0, 4, some, 0)

            last = 0
            for e in range(4):
                last = jnp.maximum(last, jnp.where(e <= yq, place_of(e), 0))

            @pl.when(last == j)
            def _():
                finish(2 * yq)
                finish(2 * yq + 1)

            return carry

        return lax.fori_loop(0, 4, one, carry)

    lax.fori_loop(0, 4, step, 0)

    for i in (3, 2, 1, 0):
        a = (y + i) % 4
        cols = head_cols(a)
        for p in range(2):
            arrived(o_in.at[a, p], o_sem.at[a, p])
            arrived(l_in.at[a, p], l_sem.at[a, p])
        l0 = home_l[a]
        l1 = jnp.broadcast_to(l_in[a, 0][:1, :], (HD, TOK)).T
        l2 = jnp.broadcast_to(l_in[a, 1][:1, :], (HD, TOK)).T
        top = jnp.maximum(jnp.maximum(l0, l1), l2)
        w0, w1, w2 = jnp.exp2(l0 - top), jnp.exp2(l1 - top), jnp.exp2(l2 - top)
        o = w0 * home[a] + w1 * o_in[a, 0].astype(f32) + w2 * o_in[a, 1].astype(f32)
        so[:, cols] = (o / (w0 + w1 + w2)).astype(bf16)

    def end(n, carry):
        for copy in o_copies(n):
            wait_sent(copy)
        return carry

    lax.fori_loop(0, 8, end, 0)
    for i in range(4):
        arrived(kv.at[i, pl.ds(0, 3)], fwd_sem.at[i])
        arrived(qb.at[i, pl.ds(0, TOK)], q_fwd.at[i])
        wait_sent(kv_copy(i, 0))
        wait_sent(kv_copy(i, 1))
        wait_sent(q_copy(i))
    arrived(st_send.at[pl.ds(0, 31 * 16)], st_ssem)
    arrived(car_send.at[pl.ds(0, 31 * 16)], car_ssem)
    arrived(ss_recv.at[pl.ds(0, 7)], ss_ssem)


def body(lq, lk, lv, lg, gain, decay_exponent, sq, sk, sv):
    log_decay = -decay_exponent.astype(f32) / 65536.0
    ld = jnp.broadcast_to(log_decay[:, None, None], (4, 8, HD))
    vmem = pl.BlockSpec(memory_space=pltpu.VMEM)
    anywhere = pl.BlockSpec(memory_space=pl.ANY)
    dma = pltpu.SemaphoreType.DMA
    local = (TOK, 4 * HD)
    out = jax.ShapeDtypeStruct(local, bf16)
    return pl.pallas_call(
        kernel,
        out_shape=(out, out),
        in_specs=[anywhere] * 4 + [vmem] * 2 + [anywhere] * 3,
        out_specs=(vmem, vmem),
        scratch_shapes=[pltpu.VMEM(local, bf16)] * 7 + [
            pltpu.VMEM((4, 4, 2, TOK, HD), bf16),
            pltpu.VMEM((4, 2 * TOK, HD), bf16),
            pltpu.VMEM((8, TOK, HD), bf16),
            pltpu.VMEM((8, 8, TOK), f32),
            pltpu.VMEM((4, 2 * TOK, HD), f32),
            pltpu.VMEM((4, 2 * TOK, 2 * HD), f32),
            pltpu.VMEM(local, f32),
            pltpu.VMEM((4, TOK, HD), f32),
            pltpu.VMEM((4, TOK, HD), f32),
            pltpu.VMEM((4, 2, TOK, HD), bf16),
            pltpu.VMEM((4, 2, 8, TOK), f32),
            pltpu.VMEM((TOK, HD), bf16),
            pltpu.VMEM((TOK, HD), bf16),
            pltpu.VMEM((TOK, HD), bf16),
            pltpu.VMEM((TOK, HD), bf16),
            pltpu.VMEM((8, TOK), f32),
            pltpu.VMEM((8, 8, TOK), f32),
            dma((7,)), dma((4, 4, 2)), dma((4, 2)), dma((8,)), dma((4,)), dma((4,)), dma((4,)),
            dma((4, 2)), dma((4, 2)), dma((8,)), dma((8,)),
            dma, dma, dma, dma, dma, dma,
        ],
        compiler_params=pltpu.CompilerParams(
            collective_id=0, has_side_effects=True, vmem_limit_bytes=62 * 1024 * 1024
        ),
        name="layers",
    )(lq, lk, lv, lg, gain[None, :], ld, sq, sk, sv)


def solution(mesh):
    spec = P("ctx", "head")
    return jax.shard_map(
        body,
        mesh=mesh,
        in_specs=(spec, spec, spec, spec, P("head"), P("head"), spec, spec, spec),
        out_specs=(spec, spec),
        check_vma=False,
    )
```

```python
import jax
import jax.numpy as jnp
from jax import lax
from jax.experimental import pallas as pl
from jax.experimental.pallas import tpu as pltpu
from jax.sharding import PartitionSpec as P

HEADS = 32
HD = 128
TOK = 512
MESH = pl.DeviceIdType.MESH
SCALE2 = HD**-0.5 * 1.4426950408889634
QT = 128
f32 = jnp.float32
bf16 = jnp.bfloat16


def dot_nt(a, b):
    return lax.dot_general(a, b, (((1,), (1,)), ((), ())), preferred_element_type=f32)


def dot_tn(a, b):
    return lax.dot_general(a, b, (((0,), (0,)), ((), ())), preferred_element_type=f32)


def kernel(
    lq_h, lk_h, lv_h, lg_h, gain, ld_ref, sq_h, sk_h, sv_h,
    lo, so,
    lq, lk, lv, lg, sq, sk, sv,
    kv, qb, ob, ol, m_ref, acc, mixed, home, home_l, o_in, l_in,
    st_send, st_recv, car_send, car_recv, ss_send, ss_recv,
    load_sem, kv_sem, p1_sem, q_sem, q_send, q_fwd, fwd_sem, o_sem, l_sem, o_send, l_send,
    st_ssem, st_rsem, car_ssem, car_rsem, ss_ssem, ss_rsem,
):
    c = lax.axis_index("ctx")
    h = lax.axis_index("head")
    y, x, zl = c // 8, (c // 2) % 4, c % 2
    zh, core = h // 2, h % 2
    sib = zh * 2 + 1 - core
    half = x // 2
    par = x % 2

    def remote(src, dst, ssem, rsem, ctx, head):
        return pltpu.make_async_remote_copy(
            src_ref=src, dst_ref=dst, send_sem=ssem, recv_sem=rsem,
            device_id=(ctx, head), device_id_type=MESH,
        )

    def arrived(ref, sem):
        pltpu.make_async_copy(ref, ref, sem).wait()

    def queries(n):
        return qb.at[n // 2, pl.ds(pl.multiple_of(n % 2 * TOK, TOK), TOK)]

    def head_cols(a):
        return pl.ds(pl.multiple_of(a * HD, HD), HD)

    barrier = pltpu.get_barrier_semaphore()

    def hello(i, carry):
        pl.semaphore_signal(
            barrier, 1,
            device_id=((c + i // 2) % 32, zh * 2 + (core + i) % 2),
            device_id_type=MESH,
        )
        return carry

    lax.fori_loop(1, 64, hello, 0)

    def hello_head(i, carry):
        pl.semaphore_signal(barrier, 1, device_id=(c, (h + i) % 8), device_id_type=MESH)
        return carry

    lax.fori_loop(2 - core, 8 - core, hello_head, 0)

    loads = [
        pltpu.make_async_copy(src, dst, load_sem.at[n])
        for n, (src, dst) in enumerate(
            ((lk_h, lk), (lv_h, lv), (lq_h, lq), (sq_h, sq), (sk_h, sk), (sv_h, sv), (lg_h, lg))
        )
    ]
    for load in loads:
        load.start()

    rows = lax.broadcasted_iota(jnp.int32, (TOK, HD), 0).astype(f32)
    loads[0].wait()
    loads[1].wait()

    for a in range(4):
        cols = pl.ds(a * HD, HD)
        ld = ld_ref[a][:1, :]
        kd = (lk[:, cols].astype(f32) * jnp.exp((TOK - 1.0 - rows) * ld)).astype(bf16)
        st_send[cols, :] = dot_tn(kd, lv[:, cols]).astype(bf16)

    m_ref[...] = jnp.full_like(m_ref, -1e30)
    acc[...] = jnp.zeros_like(acc)

    pl.semaphore_wait(barrier, 69)

    q_at = 2 * y + par

    def kv_copy(i, part):
        a = (y + i) % 4
        src = (sk_h, sv_h)[part].at[:, head_cols(a)]
        dst = kv.at[y, 2 * half + zl, part]
        sem = kv_sem.at[y, 2 * half + zl, part]
        zd = (core + a) % 2
        far = remote(src, dst, p1_sem.at[i, part], sem, a * 8 + x * 2 + zd, zh * 2 + zl)
        return (i == 0) & (zd == zl) & (core == zl), far, pltpu.make_async_copy(src, dst, sem)

    def q_copy(i):
        a = (y + i) % 4
        src = sq_h.at[:, head_cols(a)]
        dst, sem = queries(q_at), q_sem.at[q_at]
        zd = (core + a) % 2
        far = remote(src, dst, q_send.at[i], sem, a * 8 + x * 2 + zd, zh * 2 + zl)
        return (i == 0) & (zd == zl) & (core == zl), far, pltpu.make_async_copy(src, dst, sem)

    def start(copy):
        here, far, near = copy

        @pl.when(here)
        def _():
            near.start()

        @pl.when(jnp.logical_not(here))
        def _():
            far.start()

    def wait_sent(copy):
        here, far, near = copy

        @pl.when(jnp.logical_not(here))
        def _():
            far.wait_send()

    def scan_rows(i):
        return pl.ds(pl.multiple_of(i * 16, 16), 16)

    def send_state(i, carry):
        to = (c + i) % 32
        remote(st_send.at[scan_rows(to)], st_recv.at[scan_rows(c)], st_ssem, st_rsem, to, h).start()
        return carry

    lax.fori_loop(1, 32, send_state, 0)
    pltpu.make_async_copy(st_send.at[scan_rows(c)], st_recv.at[scan_rows(c)], st_rsem).start()

    start(kv_copy(0, 0))
    start(kv_copy(0, 1))
    for i in (0, 3, 2):
        start(q_copy(i))

    loads[2].wait()

    def intra(heads):
        units = [(a, i) for a in heads for i in range(2)]

        def scores(a, i):
            cols = pl.ds(a * HD, HD)
            return dot_nt(lq[pl.ds(i * 256, 256), cols], lk[pl.ds(0, (i + 1) * 256), cols])

        s = scores(*units[0])
        for at, (a, i) in enumerate(units):
            ahead = scores(*units[at + 1]) if at + 1 < len(units) else None
            n = (i + 1) * 256
            cols = pl.ds(a * HD, HD)
            ld = ld_ref[a][:1, :1]
            t = i * 256 + lax.broadcasted_iota(jnp.int32, (256, n), 0)
            j = lax.broadcasted_iota(jnp.int32, (256, n), 1)
            up = jnp.exp((i * 256 + lax.broadcasted_iota(jnp.int32, (256, 1), 0)).astype(f32) * ld)
            down = jnp.exp(-lax.broadcasted_iota(jnp.int32, (1, n), 1).astype(f32) * ld)
            w = jnp.where(t >= j, s * up * down, 0.0).astype(bf16)
            mixed[pl.ds(i * 256, 256), cols] = jnp.dot(w, lv[pl.ds(0, n), cols], preferred_element_type=f32)
            s = ahead

    intra((0, 1, 2, 3))

    start(q_copy(1))
    start(kv_copy(3, 0))
    start(kv_copy(3, 1))

    def own_piece(s):
        b = 2 * half + core
        arrived(kv.at[s, b, 0], kv_sem.at[s, b, 0])
        arrived(kv.at[s, b, 1], kv_sem.at[s, b, 1])
        remote(kv.at[s, b], kv.at[s, b], fwd_sem.at[s], kv_sem.at[s, b, 0], y * 8 + (3 - x) * 2 + zl, h).start()
        remote(kv.at[s, b], kv.at[s, b], fwd_sem.at[s], kv_sem.at[s, b, 0], c, sib).start()

    def paired_piece(s):
        b = 2 * (1 - half) + core
        arrived(kv.at[s, b], kv_sem.at[s, b, 0])
        remote(kv.at[s, b], kv.at[s, b], fwd_sem.at[s], kv_sem.at[s, b, 0], c, sib).start()

    def slice_at(j):
        return (y + jnp.where(j == 2, 3, jnp.where(j == 3, 2, j))) % 4

    def place_of(s):
        d = (s - y + 4) % 4
        return jnp.where(d == 2, 3, jnp.where(d == 3, 2, d))

    own_piece(y)

    for n in (3, 4, 5):
        loads[n].wait()

    def at_home(heads):
        units = [(a, i) for a in heads for i in range(2)]

        def scores(a, i):
            cols = pl.ds(a * HD, HD)
            return dot_nt(sq[pl.ds(i * 256, 256), cols], sk[pl.ds(0, (i + 1) * 256), cols])

        s = scores(*units[0])
        for at, (a, i) in enumerate(units):
            ahead = scores(*units[at + 1]) if at + 1 < len(units) else None
            n = (i + 1) * 256
            sl = pl.ds(i * 256, 256)
            t = i * 256 + lax.broadcasted_iota(jnp.int32, (256, n), 0)
            j = lax.broadcasted_iota(jnp.int32, (256, n), 1)
            s = jnp.where(t >= j, s, -1e30)
            top = jnp.max(s, axis=1, keepdims=True)
            p = jnp.exp2((s - top) * SCALE2).astype(bf16)
            v = sv[pl.ds(0, n), pl.ds(a * HD, HD)]
            o = jnp.dot(p, jnp.concatenate([v, jnp.ones_like(v)], axis=1), preferred_element_type=f32)
            home[a, sl, :] = o[:, :HD] / o[:, HD:]
            home_l[a, sl, :] = top * SCALE2 + jnp.log2(o[:, HD:])
            s = ahead

    def pass_queries(i):
        yq = (y + i) % 4
        n = 2 * yq + par
        arrived(queries(n), q_sem.at[n])
        remote(queries(n), queries(n), q_fwd.at[i], q_sem.at[n], y * 8 + (x + 1 - 2 * par) * 2 + zl, h).start()

    at_home((0, 1))
    start(kv_copy(1, 0))
    start(kv_copy(1, 1))
    pass_queries(0)
    pass_queries(1)
    at_home((2, 3))
    start(kv_copy(2, 0))
    start(kv_copy(2, 1))
    pass_queries(2)
    pass_queries(3)

    def scan_states():
        arrived(st_recv, st_rsem)
        f = jnp.exp(TOK * ld_ref[c // 8][:1, :])

        def step(b, carry):
            car_send[scan_rows(b), :] = carry.astype(bf16)
            return carry * f + st_recv[scan_rows(b), :].astype(f32)

        lax.fori_loop(0, 32, step, jnp.zeros((16, HD), f32))

        def send_carried(i, carry):
            to = (c + i) % 32
            remote(car_send.at[scan_rows(to)], car_recv.at[scan_rows(c)], car_ssem, car_rsem, to, h).start()
            return carry

        lax.fori_loop(1, 32, send_carried, 0)
        pltpu.make_async_copy(car_send.at[scan_rows(c)], car_recv.at[scan_rows(c)], car_rsem).start()

    def add_inter():
        arrived(car_recv, car_rsem)

        def one(a, squares):
            cols = head_cols(a)
            ld = ld_ref[a][:1, :]
            inter = jnp.dot(lq[:, cols], car_recv[head_cols(a), :], preferred_element_type=f32)
            both = mixed[:, cols] + jnp.exp((rows + 1.0) * ld) * inter
            mixed[:, cols] = both
            return squares + both * both

        squares = lax.fori_loop(0, 4, one, jnp.zeros((TOK, HD), f32))
        total = jnp.sum(squares.T, axis=0, keepdims=True)
        ss_send[...] = jnp.broadcast_to(total, (8, TOK))
        ss_recv[h] = ss_send[...]

        def send_squares(i, carry):
            remote(ss_send, ss_recv.at[h], ss_ssem, ss_rsem, c, (h + i) % 8).start()
            return carry

        lax.fori_loop(1, 8, send_squares, 0)

    def finish_light():
        arrived(ss_recv.at[pl.ds(0, 7)], ss_rsem)
        loads[6].wait()
        total = jnp.sum(ss_recv[...], axis=0)[:1, :]
        scale = lax.rsqrt(total / (HEADS * HD) + 1e-5)
        scale = jnp.broadcast_to(scale, (HD, TOK)).T
        for a in range(4):
            cols = pl.ds(a * HD, HD)
            gate = lg[:, cols].astype(f32)
            lo[:, cols] = (mixed[:, cols] * scale * gain[:, cols] / (1.0 + jnp.exp(-gate))).astype(bf16)


    own_piece(slice_at(1))

    def tile(k, v, yq, start_row, count):
        v2 = jnp.concatenate([v, jnp.ones_like(v)], axis=1)

        def piece(i):
            return pl.ds(start_row + i * QT, QT)

        def scores(i):
            return dot_nt(qb[yq, piece(i), :], k)

        def add(i, p, shrink):
            acc[yq, piece(i), :] = acc[yq, piece(i), :] * jnp.concatenate([shrink, shrink], axis=1) + jnp.dot(
                p, v2, preferred_element_type=f32
            )

        s = scores(0)
        behind = None
        for i in range(count // QT):
            ahead = scores(i + 1) if (i + 1) * QT < count else None
            old = m_ref[yq, piece(i), :]
            new = jnp.maximum(old, jnp.max(s, axis=1, keepdims=True))
            p = jnp.exp2((s - new[:, :1]) * SCALE2).astype(bf16)
            shrink = jnp.exp2((old - new) * SCALE2)
            m_ref[yq, piece(i), :] = new
            if behind is not None:
                add(*behind)
            behind = (i, p, shrink)
            s = ahead
        add(*behind)

    def query_home(n):
        return 2 * half + n % 2, core

    def o_copies(n):
        yq = n // 2
        ox, oz = query_home(n)
        from_core = (zl + y) % 2
        here = (yq == y) & (ox == x) & (oz == zl) & (core == from_core)
        ctx, head = yq * 8 + ox * 2 + oz, zh * 2 + from_core
        return [
            (here, remote(src.at[n], dst.at[y, par], ssem.at[n], rsem.at[y, par], ctx, head),
             pltpu.make_async_copy(src.at[n], dst.at[y, par], rsem.at[y, par]))
            for src, dst, ssem, rsem in ((ob, o_in, o_send, o_sem), (ol, l_in, l_send, l_sem))
        ]

    def finish(n):
        yq, base = n // 2, pl.multiple_of(n % 2 * TOK, TOK)
        for i in range(2):
            sl, at = pl.ds(i * 256, 256), pl.ds(base + i * 256, 256)
            total = acc[yq, at, HD:]
            some = jnp.maximum(total, 1e-30)
            ob[n, sl, :] = (acc[yq, at, :HD] / some).astype(bf16)
            lse = jnp.where(total > 0.0, m_ref[yq, at, :] * SCALE2 + jnp.log2(some), -1e30)
            ol[n, :, sl] = lse.T[:8, :]
        for copy in o_copies(n):
            start(copy)

    paired_piece(y)

    def step(j, carry):
        s = slice_at(j)
        for part in range(2):
            b = 2 * part + 1 - core
            arrived(kv.at[s, b], kv_sem.at[s, b, 0])

        def one(i, carry):
            yq = (y + 1 + i) % 4

            @pl.when(j == 0)
            def _():
                n = 2 * yq + 1 - par
                arrived(queries(n), q_sem.at[n])

            @pl.when((i == 1) & (j < 2))
            def _():
                own_piece(slice_at(j + 2))

            @pl.when((i == 3) & (j < 3))
            def _():
                paired_piece(slice_at(j + 1))

            @pl.when((i == 2) & (j == 0))
            def _():
                scan_states()

            @pl.when((i == 2) & (j == 1))
            def _():
                add_inter()

            @pl.when((i == 2) & (j == 3))
            def _():
                finish_light()

            @pl.when(s < yq)
            def _():
                k = kv[s, :, 0].reshape(4 * TOK, HD)
                v = kv[s, :, 1].reshape(4 * TOK, HD)
                tile(k, v, yq, 0, 2 * TOK)

            @pl.when(s == yq)
            def _():
                def some(e, carry):
                    n, at = 2 * yq + e // 2, e % 2
                    xk = jnp.where(at == half, x, 3 - x)
                    row = pl.multiple_of(e // 2 * TOK, TOK)
                    ox, oz = query_home(n)

                    @pl.when(xk < ox)
                    def _():
                        k = kv[s, pl.ds(2 * at, 2), 0].reshape(2 * TOK, HD)
                        v = kv[s, pl.ds(2 * at, 2), 1].reshape(2 * TOK, HD)
                        tile(k, v, yq, row, TOK)

                    @pl.when((xk == ox) & (oz == 1))
                    def _():
                        tile(kv[s, 2 * at, 0], kv[s, 2 * at, 1], yq, row, TOK)

                    return carry

                lax.fori_loop(0, 4, some, 0)

            last = 0
            for e in range(4):
                last = jnp.maximum(last, jnp.where(e <= yq, place_of(e), 0))

            @pl.when(last == j)
            def _():
                finish(2 * yq)
                finish(2 * yq + 1)

            return carry

        return lax.fori_loop(0, 4, one, carry)

    lax.fori_loop(0, 4, step, 0)

    for i in (3, 2, 1, 0):
        a = (y + i) % 4
        cols = head_cols(a)
        for p in range(2):
            arrived(o_in.at[a, p], o_sem.at[a, p])
            arrived(l_in.at[a, p], l_sem.at[a, p])
        l0 = home_l[a]
        l1 = jnp.broadcast_to(l_in[a, 0][:1, :], (HD, TOK)).T
        l2 = jnp.broadcast_to(l_in[a, 1][:1, :], (HD, TOK)).T
        top = jnp.maximum(jnp.maximum(l0, l1), l2)
        w0, w1, w2 = jnp.exp2(l0 - top), jnp.exp2(l1 - top), jnp.exp2(l2 - top)
        o = w0 * home[a] + w1 * o_in[a, 0].astype(f32) + w2 * o_in[a, 1].astype(f32)
        so[:, cols] = (o / (w0 + w1 + w2)).astype(bf16)

    def end(n, carry):
        for copy in o_copies(n):
            wait_sent(copy)
        return carry

    lax.fori_loop(0, 8, end, 0)
    for i in range(4):
        arrived(kv.at[i, pl.ds(0, 3)], fwd_sem.at[i])
        arrived(qb.at[i, pl.ds(0, TOK)], q_fwd.at[i])
        wait_sent(kv_copy(i, 0))
        wait_sent(kv_copy(i, 1))
        wait_sent(q_copy(i))
    arrived(st_send.at[pl.ds(0, 31 * 16)], st_ssem)
    arrived(car_send.at[pl.ds(0, 31 * 16)], car_ssem)
    arrived(ss_recv.at[pl.ds(0, 7)], ss_ssem)


def body(lq, lk, lv, lg, gain, decay_exponent, sq, sk, sv):
    log_decay = -decay_exponent.astype(f32) / 65536.0
    ld = jnp.broadcast_to(log_decay[:, None, None], (4, 8, HD))
    vmem = pl.BlockSpec(memory_space=pltpu.VMEM)
    anywhere = pl.BlockSpec(memory_space=pl.ANY)
    dma = pltpu.SemaphoreType.DMA
    local = (TOK, 4 * HD)
    out = jax.ShapeDtypeStruct(local, bf16)
    return pl.pallas_call(
        kernel,
        out_shape=(out, out),
        in_specs=[anywhere] * 4 + [vmem] * 2 + [anywhere] * 3,
        out_specs=(vmem, vmem),
        scratch_shapes=[pltpu.VMEM(local, bf16)] * 7 + [
            pltpu.VMEM((4, 4, 2, TOK, HD), bf16),
            pltpu.VMEM((4, 2 * TOK, HD), bf16),
            pltpu.VMEM((8, TOK, HD), bf16),
            pltpu.VMEM((8, 8, TOK), f32),
            pltpu.VMEM((4, 2 * TOK, HD), f32),
            pltpu.VMEM((4, 2 * TOK, 2 * HD), f32),
            pltpu.VMEM(local, f32),
            pltpu.VMEM((4, TOK, HD), f32),
            pltpu.VMEM((4, TOK, HD), f32),
            pltpu.VMEM((4, 2, TOK, HD), bf16),
            pltpu.VMEM((4, 2, 8, TOK), f32),
            pltpu.VMEM((TOK, HD), bf16),
            pltpu.VMEM((TOK, HD), bf16),
            pltpu.VMEM((TOK, HD), bf16),
            pltpu.VMEM((TOK, HD), bf16),
            pltpu.VMEM((8, TOK), f32),
            pltpu.VMEM((8, 8, TOK), f32),
            dma((7,)), dma((4, 4, 2)), dma((4, 2)), dma((8,)), dma((4,)), dma((4,)), dma((4,)),
            dma((4, 2)), dma((4, 2)), dma((8,)), dma((8,)),
            dma, dma, dma, dma, dma, dma,
        ],
        compiler_params=pltpu.CompilerParams(
            collective_id=0, has_side_effects=True, vmem_limit_bytes=62 * 1024 * 1024
        ),
        name="layers",
    )(lq, lk, lv, lg, gain[None, :], ld, sq, sk, sv)


def solution(mesh):
    spec = P("ctx", "head")
    return jax.shard_map(
        body,
        mesh=mesh,
        in_specs=(spec, spec, spec, spec, P("head"), P("head"), spec, spec, spec),
        out_specs=(spec, spec),
        check_vma=False,
    )
```

```python
import jax
import jax.numpy as jnp
from jax import lax
from jax.experimental import pallas as pl
from jax.experimental.pallas import tpu as pltpu
from jax.sharding import PartitionSpec as P

HEADS = 32
HD = 128
TOK = 512
MESH = pl.DeviceIdType.MESH
SCALE2 = HD**-0.5 * 1.4426950408889634
QT = 128
f32 = jnp.float32
bf16 = jnp.bfloat16


def dot_nt(a, b):
    return lax.dot_general(a, b, (((1,), (1,)), ((), ())), preferred_element_type=f32)


def dot_tn(a, b):
    return lax.dot_general(a, b, (((0,), (0,)), ((), ())), preferred_element_type=f32)


def kernel(
    lq_h, lk_h, lv_h, lg_h, gain, exponent, sq_h, sk_h, sv_h,
    lo, so,
    lq, lk, lv, lg, sq, sk, sv,
    kv, qb, ob, ol, m_ref, acc, mixed, home, home_l, o_in, l_in,
    st_send, st_recv, car_send, car_recv, ss_send, ss_recv,
    load_sem, kv_sem, p1_sem, q_sem, q_send, q_fwd, fwd_sem, o_sem, l_sem, o_send, l_send,
    st_ssem, st_rsem, car_ssem, car_rsem, ss_ssem, ss_rsem,
):
    c = lax.axis_index("ctx")
    h = lax.axis_index("head")
    y, x, zl = c // 8, (c // 2) % 4, c % 2
    zh, core = h // 2, h % 2
    sib = zh * 2 + 1 - core
    half = x // 2
    par = x % 2

    def remote(src, dst, ssem, rsem, ctx, head):
        return pltpu.make_async_remote_copy(
            src_ref=src, dst_ref=dst, send_sem=ssem, recv_sem=rsem,
            device_id=(ctx, head), device_id_type=MESH,
        )

    def arrived(ref, sem):
        pltpu.make_async_copy(ref, ref, sem).wait()

    def queries(n):
        return qb.at[n // 2, pl.ds(pl.multiple_of(n % 2 * TOK, TOK), TOK)]

    def log_decay(a):
        return jnp.full((1, HD), exponent[a], jnp.int32).astype(f32) * (-1.0 / 65536.0)

    def head_cols(a):
        return pl.ds(pl.multiple_of(a * HD, HD), HD)

    barrier = pltpu.get_barrier_semaphore()

    def hello(i, carry):
        pl.semaphore_signal(
            barrier, 1,
            device_id=((c + i // 2) % 32, zh * 2 + (core + i) % 2),
            device_id_type=MESH,
        )
        return carry

    lax.fori_loop(1, 64, hello, 0)

    def hello_head(i, carry):
        pl.semaphore_signal(barrier, 1, device_id=(c, (h + i) % 8), device_id_type=MESH)
        return carry

    lax.fori_loop(2 - core, 8 - core, hello_head, 0)

    loads = [
        pltpu.make_async_copy(src, dst, load_sem.at[n])
        for n, (src, dst) in enumerate(
            ((lk_h, lk), (lv_h, lv), (lq_h, lq), (sq_h, sq), (sk_h, sk), (sv_h, sv), (lg_h, lg))
        )
    ]
    for load in loads:
        load.start()

    rows = lax.broadcasted_iota(jnp.int32, (TOK, HD), 0).astype(f32)
    loads[0].wait()
    loads[1].wait()

    for a in range(4):
        cols = pl.ds(a * HD, HD)
        ld = log_decay(a)
        kd = (lk[:, cols].astype(f32) * jnp.exp((TOK - 1.0 - rows) * ld)).astype(bf16)
        st_send[cols, :] = dot_tn(kd, lv[:, cols]).astype(bf16)

    m_ref[...] = jnp.full_like(m_ref, -1e30)
    acc[...] = jnp.zeros_like(acc)

    pl.semaphore_wait(barrier, 69)

    q_at = 2 * y + par

    def kv_copy(i, part):
        a = (y + i) % 4
        src = (sk_h, sv_h)[part].at[:, head_cols(a)]
        dst = kv.at[y, 2 * half + zl, part]
        sem = kv_sem.at[y, 2 * half + zl, part]
        zd = (core + a) % 2
        far = remote(src, dst, p1_sem.at[i, part], sem, a * 8 + x * 2 + zd, zh * 2 + zl)
        return (i == 0) & (zd == zl) & (core == zl), far, pltpu.make_async_copy(src, dst, sem)

    def q_copy(i):
        a = (y + i) % 4
        src = sq_h.at[:, head_cols(a)]
        dst, sem = queries(q_at), q_sem.at[q_at]
        zd = (core + a) % 2
        far = remote(src, dst, q_send.at[i], sem, a * 8 + x * 2 + zd, zh * 2 + zl)
        return (i == 0) & (zd == zl) & (core == zl), far, pltpu.make_async_copy(src, dst, sem)

    def start(copy):
        here, far, near = copy

        @pl.when(here)
        def _():
            near.start()

        @pl.when(jnp.logical_not(here))
        def _():
            far.start()

    def wait_sent(copy):
        here, far, near = copy

        @pl.when(jnp.logical_not(here))
        def _():
            far.wait_send()

    def scan_rows(i):
        return pl.ds(pl.multiple_of(i * 16, 16), 16)

    def send_state(i, carry):
        to = (c + i) % 32
        remote(st_send.at[scan_rows(to)], st_recv.at[scan_rows(c)], st_ssem, st_rsem, to, h).start()
        return carry

    lax.fori_loop(1, 32, send_state, 0)
    pltpu.make_async_copy(st_send.at[scan_rows(c)], st_recv.at[scan_rows(c)], st_rsem).start()

    start(kv_copy(0, 0))
    start(kv_copy(0, 1))
    for i in (0, 3, 2):
        start(q_copy(i))

    loads[2].wait()

    def intra(heads):
        units = [(a, i) for a in heads for i in range(2)]

        def scores(a, i):
            cols = pl.ds(a * HD, HD)
            return dot_nt(lq[pl.ds(i * 256, 256), cols], lk[pl.ds(0, (i + 1) * 256), cols])

        s = scores(*units[0])
        for at, (a, i) in enumerate(units):
            ahead = scores(*units[at + 1]) if at + 1 < len(units) else None
            n = (i + 1) * 256
            cols = pl.ds(a * HD, HD)
            ld = log_decay(a)[:, :1]
            t = i * 256 + lax.broadcasted_iota(jnp.int32, (256, n), 0)
            j = lax.broadcasted_iota(jnp.int32, (256, n), 1)
            up = jnp.exp((i * 256 + lax.broadcasted_iota(jnp.int32, (256, 1), 0)).astype(f32) * ld)
            down = jnp.exp(-lax.broadcasted_iota(jnp.int32, (1, n), 1).astype(f32) * ld)
            w = jnp.where(t >= j, s * up * down, 0.0).astype(bf16)
            mixed[pl.ds(i * 256, 256), cols] = jnp.dot(w, lv[pl.ds(0, n), cols], preferred_element_type=f32)
            s = ahead

    intra((0, 1, 2, 3))

    start(q_copy(1))
    start(kv_copy(3, 0))
    start(kv_copy(3, 1))

    def own_piece(s):
        b = 2 * half + core
        arrived(kv.at[s, b, 0], kv_sem.at[s, b, 0])
        arrived(kv.at[s, b, 1], kv_sem.at[s, b, 1])
        remote(kv.at[s, b], kv.at[s, b], fwd_sem.at[s], kv_sem.at[s, b, 0], y * 8 + (3 - x) * 2 + zl, h).start()
        remote(kv.at[s, b], kv.at[s, b], fwd_sem.at[s], kv_sem.at[s, b, 0], c, sib).start()

    def paired_piece(s):
        b = 2 * (1 - half) + core
        arrived(kv.at[s, b], kv_sem.at[s, b, 0])
        remote(kv.at[s, b], kv.at[s, b], fwd_sem.at[s], kv_sem.at[s, b, 0], c, sib).start()

    def slice_at(j):
        return (y + jnp.where(j == 2, 3, jnp.where(j == 3, 2, j))) % 4

    def place_of(s):
        d = (s - y + 4) % 4
        return jnp.where(d == 2, 3, jnp.where(d == 3, 2, d))

    own_piece(y)

    for n in (3, 4, 5):
        loads[n].wait()

    def at_home(heads):
        units = [(a, i) for a in heads for i in range(2)]

        def scores(a, i):
            cols = pl.ds(a * HD, HD)
            return dot_nt(sq[pl.ds(i * 256, 256), cols], sk[pl.ds(0, (i + 1) * 256), cols])

        s = scores(*units[0])
        for at, (a, i) in enumerate(units):
            ahead = scores(*units[at + 1]) if at + 1 < len(units) else None
            n = (i + 1) * 256
            sl = pl.ds(i * 256, 256)
            t = i * 256 + lax.broadcasted_iota(jnp.int32, (256, n), 0)
            j = lax.broadcasted_iota(jnp.int32, (256, n), 1)
            s = jnp.where(t >= j, s, -1e30)
            top = jnp.max(s, axis=1, keepdims=True)
            p = jnp.exp2((s - top) * SCALE2).astype(bf16)
            v = sv[pl.ds(0, n), pl.ds(a * HD, HD)]
            o = jnp.dot(p, jnp.concatenate([v, jnp.ones_like(v)], axis=1), preferred_element_type=f32)
            home[a, sl, :] = o[:, :HD] / o[:, HD:]
            home_l[a, sl, :] = top * SCALE2 + jnp.log2(o[:, HD:])
            s = ahead

    def pass_queries(i):
        yq = (y + i) % 4
        n = 2 * yq + par
        arrived(queries(n), q_sem.at[n])
        remote(queries(n), queries(n), q_fwd.at[i], q_sem.at[n], y * 8 + (x + 1 - 2 * par) * 2 + zl, h).start()

    at_home((0, 1))
    start(kv_copy(1, 0))
    start(kv_copy(1, 1))
    pass_queries(0)
    pass_queries(1)
    at_home((2, 3))
    start(kv_copy(2, 0))
    start(kv_copy(2, 1))
    pass_queries(2)
    pass_queries(3)

    def scan_states():
        arrived(st_recv, st_rsem)
        f = jnp.exp(TOK * log_decay(c // 8))

        def step(b, carry):
            car_send[scan_rows(b), :] = carry.astype(bf16)
            return carry * f + st_recv[scan_rows(b), :].astype(f32)

        lax.fori_loop(0, 32, step, jnp.zeros((16, HD), f32))

        def send_carried(i, carry):
            to = (c + i) % 32
            remote(car_send.at[scan_rows(to)], car_recv.at[scan_rows(c)], car_ssem, car_rsem, to, h).start()
            return carry

        lax.fori_loop(1, 32, send_carried, 0)
        pltpu.make_async_copy(car_send.at[scan_rows(c)], car_recv.at[scan_rows(c)], car_rsem).start()

    def add_inter():
        arrived(car_recv, car_rsem)

        def one(a, squares):
            cols = head_cols(a)
            ld = log_decay(a)
            inter = jnp.dot(lq[:, cols], car_recv[head_cols(a), :], preferred_element_type=f32)
            both = mixed[:, cols] + jnp.exp((rows + 1.0) * ld) * inter
            mixed[:, cols] = both
            return squares + both * both

        squares = lax.fori_loop(0, 4, one, jnp.zeros((TOK, HD), f32))
        total = jnp.sum(squares.T, axis=0, keepdims=True)
        ss_send[...] = jnp.broadcast_to(total, (8, TOK))
        ss_recv[h] = ss_send[...]

        def send_squares(i, carry):
            remote(ss_send, ss_recv.at[h], ss_ssem, ss_rsem, c, (h + i) % 8).start()
            return carry

        lax.fori_loop(1, 8, send_squares, 0)

    def finish_light():
        arrived(ss_recv.at[pl.ds(0, 7)], ss_rsem)
        loads[6].wait()
        total = jnp.sum(ss_recv[...], axis=0)[:1, :]
        scale = lax.rsqrt(total / (HEADS * HD) + 1e-5)
        scale = jnp.broadcast_to(scale, (HD, TOK)).T
        for a in range(4):
            cols = pl.ds(a * HD, HD)
            gate = lg[:, cols].astype(f32)
            lo[:, cols] = (mixed[:, cols] * scale * gain[:, cols] / (1.0 + jnp.exp(-gate))).astype(bf16)


    own_piece(slice_at(1))

    def tile(k, v, yq, start_row, count):
        v2 = jnp.concatenate([v, jnp.ones_like(v)], axis=1)

        def piece(i):
            return pl.ds(start_row + i * QT, QT)

        def scores(i):
            return dot_nt(qb[yq, piece(i), :], k)

        def add(i, p, shrink):
            acc[yq, piece(i), :] = acc[yq, piece(i), :] * jnp.concatenate([shrink, shrink], axis=1) + jnp.dot(
                p, v2, preferred_element_type=f32
            )

        s = scores(0)
        behind = None
        for i in range(count // QT):
            ahead = scores(i + 1) if (i + 1) * QT < count else None
            old = m_ref[yq, piece(i), :]
            new = jnp.maximum(old, jnp.max(s, axis=1, keepdims=True))
            p = jnp.exp2((s - new[:, :1]) * SCALE2).astype(bf16)
            shrink = jnp.exp2((old - new) * SCALE2)
            m_ref[yq, piece(i), :] = new
            if behind is not None:
                add(*behind)
            behind = (i, p, shrink)
            s = ahead
        add(*behind)

    def query_home(n):
        return 2 * half + n % 2, core

    def o_copies(n):
        yq = n // 2
        ox, oz = query_home(n)
        from_core = (zl + y) % 2
        here = (yq == y) & (ox == x) & (oz == zl) & (core == from_core)
        ctx, head = yq * 8 + ox * 2 + oz, zh * 2 + from_core
        return [
            (here, remote(src.at[n], dst.at[y, par], ssem.at[n], rsem.at[y, par], ctx, head),
             pltpu.make_async_copy(src.at[n], dst.at[y, par], rsem.at[y, par]))
            for src, dst, ssem, rsem in ((ob, o_in, o_send, o_sem), (ol, l_in, l_send, l_sem))
        ]

    def finish(n):
        yq, base = n // 2, pl.multiple_of(n % 2 * TOK, TOK)
        for i in range(2):
            sl, at = pl.ds(i * 256, 256), pl.ds(base + i * 256, 256)
            total = acc[yq, at, HD:]
            some = jnp.maximum(total, 1e-30)
            ob[n, sl, :] = (acc[yq, at, :HD] / some).astype(bf16)
            lse = jnp.where(total > 0.0, m_ref[yq, at, :] * SCALE2 + jnp.log2(some), -1e30)
            ol[n, :, sl] = lse.T[:8, :]
        for copy in o_copies(n):
            start(copy)

    paired_piece(y)

    def step(j, carry):
        s = slice_at(j)
        for part in range(2):
            b = 2 * part + 1 - core
            arrived(kv.at[s, b], kv_sem.at[s, b, 0])

        def one(i, carry):
            yq = (y + 1 + i) % 4

            @pl.when(j == 0)
            def _():
                n = 2 * yq + 1 - par
                arrived(queries(n), q_sem.at[n])

            @pl.when((i == 1) & (j < 2))
            def _():
                own_piece(slice_at(j + 2))

            @pl.when((i == 3) & (j < 3))
            def _():
                paired_piece(slice_at(j + 1))

            @pl.when((i == 2) & (j == 0))
            def _():
                scan_states()

            @pl.when((i == 2) & (j == 1))
            def _():
                add_inter()

            @pl.when((i == 2) & (j == 3))
            def _():
                finish_light()

            @pl.when(s < yq)
            def _():
                k = kv[s, :, 0].reshape(4 * TOK, HD)
                v = kv[s, :, 1].reshape(4 * TOK, HD)
                tile(k, v, yq, 0, 2 * TOK)

            @pl.when(s == yq)
            def _():
                def some(e, carry):
                    n, at = 2 * yq + e // 2, e % 2
                    xk = jnp.where(at == half, x, 3 - x)
                    row = pl.multiple_of(e // 2 * TOK, TOK)
                    ox, oz = query_home(n)

                    @pl.when(xk < ox)
                    def _():
                        k = kv[s, pl.ds(2 * at, 2), 0].reshape(2 * TOK, HD)
                        v = kv[s, pl.ds(2 * at, 2), 1].reshape(2 * TOK, HD)
                        tile(k, v, yq, row, TOK)

                    @pl.when((xk == ox) & (oz == 1))
                    def _():
                        tile(kv[s, 2 * at, 0], kv[s, 2 * at, 1], yq, row, TOK)

                    return carry

                lax.fori_loop(0, 4, some, 0)

            last = 0
            for e in range(4):
                last = jnp.maximum(last, jnp.where(e <= yq, place_of(e), 0))

            @pl.when(last == j)
            def _():
                finish(2 * yq)
                finish(2 * yq + 1)

            return carry

        return lax.fori_loop(0, 4, one, carry)

    lax.fori_loop(0, 4, step, 0)

    for i in (3, 2, 1, 0):
        a = (y + i) % 4
        cols = head_cols(a)
        for p in range(2):
            arrived(o_in.at[a, p], o_sem.at[a, p])
            arrived(l_in.at[a, p], l_sem.at[a, p])
        l0 = home_l[a]
        l1 = jnp.broadcast_to(l_in[a, 0][:1, :], (HD, TOK)).T
        l2 = jnp.broadcast_to(l_in[a, 1][:1, :], (HD, TOK)).T
        top = jnp.maximum(jnp.maximum(l0, l1), l2)
        w0, w1, w2 = jnp.exp2(l0 - top), jnp.exp2(l1 - top), jnp.exp2(l2 - top)
        o = w0 * home[a] + w1 * o_in[a, 0].astype(f32) + w2 * o_in[a, 1].astype(f32)
        so[:, cols] = (o / (w0 + w1 + w2)).astype(bf16)

    def end(n, carry):
        for copy in o_copies(n):
            wait_sent(copy)
        return carry

    lax.fori_loop(0, 8, end, 0)
    for i in range(4):
        arrived(kv.at[i, pl.ds(0, 3)], fwd_sem.at[i])
        arrived(qb.at[i, pl.ds(0, TOK)], q_fwd.at[i])
        wait_sent(kv_copy(i, 0))
        wait_sent(kv_copy(i, 1))
        wait_sent(q_copy(i))
    arrived(st_send.at[pl.ds(0, 31 * 16)], st_ssem)
    arrived(car_send.at[pl.ds(0, 31 * 16)], car_ssem)
    arrived(ss_recv.at[pl.ds(0, 7)], ss_ssem)


def body(lq, lk, lv, lg, gain, decay_exponent, sq, sk, sv):
    vmem = pl.BlockSpec(memory_space=pltpu.VMEM)
    anywhere = pl.BlockSpec(memory_space=pl.ANY)
    dma = pltpu.SemaphoreType.DMA
    local = (TOK, 4 * HD)
    smem = pl.BlockSpec(memory_space=pltpu.SMEM)
    out = jax.ShapeDtypeStruct(local, bf16)
    return pl.pallas_call(
        kernel,
        out_shape=(out, out),
        in_specs=[anywhere] * 4 + [vmem, smem] + [anywhere] * 3,
        out_specs=(vmem, vmem),
        scratch_shapes=[pltpu.VMEM(local, bf16)] * 7 + [
            pltpu.VMEM((4, 4, 2, TOK, HD), bf16),
            pltpu.VMEM((4, 2 * TOK, HD), bf16),
            pltpu.VMEM((8, TOK, HD), bf16),
            pltpu.VMEM((8, 8, TOK), f32),
            pltpu.VMEM((4, 2 * TOK, HD), f32),
            pltpu.VMEM((4, 2 * TOK, 2 * HD), f32),
            pltpu.VMEM(local, f32),
            pltpu.VMEM((4, TOK, HD), f32),
            pltpu.VMEM((4, TOK, HD), f32),
            pltpu.VMEM((4, 2, TOK, HD), bf16),
            pltpu.VMEM((4, 2, 8, TOK), f32),
            pltpu.VMEM((TOK, HD), bf16),
            pltpu.VMEM((TOK, HD), bf16),
            pltpu.VMEM((TOK, HD), bf16),
            pltpu.VMEM((TOK, HD), bf16),
            pltpu.VMEM((8, TOK), f32),
            pltpu.VMEM((8, 8, TOK), f32),
            dma((7,)), dma((4, 4, 2)), dma((4, 2)), dma((8,)), dma((4,)), dma((4,)), dma((4,)),
            dma((4, 2)), dma((4, 2)), dma((8,)), dma((8,)),
            dma, dma, dma, dma, dma, dma,
        ],
        compiler_params=pltpu.CompilerParams(
            collective_id=0, has_side_effects=True, vmem_limit_bytes=62 * 1024 * 1024
        ),
        name="layers",
    )(lq, lk, lv, lg, gain[None, :], decay_exponent, sq, sk, sv)


def solution(mesh):
    spec = P("ctx", "head")
    return jax.shard_map(
        body,
        mesh=mesh,
        in_specs=(spec, spec, spec, spec, P("head"), P("head"), spec, spec, spec),
        out_specs=(spec, spec),
        check_vma=False,
    )
```
